32 devices in a mesh: ens: 2 (over x), lat: 16 (over z, y, core).
Axes of the slice: x: 2, y: 2, z: 4, core: 2. Of those that a mesh axis runs over, the one named last changes fastest.
Arguments:
- field_in: bfloat16 [512, 64, 1440], P('ens', 'lat'), parts along dimension 0, may hold values from -6 to 6
- filter_weight: bfloat16 [512, 9, 256], replicated, may hold values from -0.125 to 0.125
- filter_basis: bfloat16 [32, 9, 5, 33], P('lat'), may hold values from -0.71875 to 0.71875
- halo_reach: int32 [32], P('lat'), may hold values from 1 to 16, as said below
- grad_out: bfloat16 [1024, 32, 720], P('ens', 'lat'), parts along dimension 0, may hold values from -6 to 6
Outputs:
- field_out: bfloat16 [1024, 32, 720], P('ens', 'lat'), parts along dimension 0
- grad_in: bfloat16 [512, 64, 1440], P('ens', 'lat'), parts along dimension 0
- grad_weight: float32 [1024, 9, 256], P('ens'), parts along dimension 0
The draws below stay inside these ranges and needn't reach their ends.
There are 2 independent parts, one for each index of `ens`. The reference program is written for one: setup_inputs(seed, part) draws one part's arguments, and reference() takes and returns one part's arrays. A program takes and returns all parts, laid end to end along the dimension named above; an argument that names none is the same for every part. Nothing has to cross between parts.
Inputs may be any that keep to these rules, and one draw needn't show every extreme that they name: `halo_reach`: some output row reaches 16.
All inputs are finite; a program needn't handle non-finite values.
Results may differ from the reference program's by a relative error of at most 0.0049.
Values may be sent and summed in bfloat16 or wider, within the bound.
A program may use at most 192 MiB of HBM per device.

```python
import math
import jax
import jax.numpy as jnp
from jax import lax

CI = 256
CO = 512
KERNELS = 9
HALO = 16
NLON_OUT = 720
NLON_IN = 1440
NLAT_OUT = 32
NLAT_IN = 64


def draw_halo_reach(key, part):
    first_key = jax.random.fold_in(key, 11)
    second_key = jax.random.fold_in(key, 12)
    values = jax.random.randint(first_key, (NLAT_OUT,), 1, HALO + 1, dtype=jnp.int32)
    chosen = jax.random.randint(second_key, (), 0, NLAT_OUT, dtype=jnp.int32)
    places = jnp.arange(NLAT_OUT, dtype=jnp.int32)
    return jnp.where(places == chosen, HALO, values).astype(jnp.int32)


def level_of(rng, dims, split, least, high):
    gain, own = 1.0, jax.random.fold_in(rng, 6)
    for position, parts in split:
        heights = jnp.exp(jax.random.uniform(jax.random.fold_in(own, position), (parts,), jnp.float32, least / len(split), high / len(split)))
        gain = gain * jnp.repeat(heights, dims[position] // parts).reshape([-1 if axis == position else 1 for axis in range(len(dims))])
    return gain


def bell_draw(stream_key, shape, spread, limit, split=(), held_as=jnp.bfloat16):
    level = level_of(stream_key, shape, split, -0.22, 0.18) if split else 1.0
    result = jax.random.normal(stream_key, shape, jnp.float32) * spread * level
    return jnp.minimum(jnp.maximum(result, -limit), limit).astype(held_as)


def setup_inputs(seed: int = 0, part: int = 0) -> dict:
    seeds = jax.random.split(jax.random.key(seed), 6)
    part_keys = jax.random.split(jax.random.fold_in(seeds[5], part), 6)
    field_in = bell_draw(part_keys[0], (CI, NLAT_IN, NLON_IN), 1.0, 6.0, ((1, 16),))
    filter_weight = bell_draw(seeds[1], (CO, KERNELS, CI), (KERNELS * CI) ** -0.5, 0.125)
    filter_basis = bell_draw(seeds[2], (NLAT_OUT, KERNELS, 5, 2 * HALO + 1), 0.12, 0.71875, ((0, 16),))
    halo_reach = draw_halo_reach(jax.random.fold_in(seeds[5], 71), part)
    grad_out = bell_draw(part_keys[4], (CO, NLAT_OUT, NLON_OUT), 1.0, 6.0, ((1, 16),))
    return dict(field_in=field_in, filter_weight=filter_weight, filter_basis=filter_basis, halo_reach=halo_reach, grad_out=grad_out)


def stencil(field32, masked32):
    padded = jnp.pad(field32, ((0, 0), (2, 2), (0, 0)))
    lon_index = (2 * jnp.arange(NLON_OUT, dtype=jnp.int32)[:, None] + jnp.arange(2 * HALO + 1, dtype=jnp.int32)[None, :] - HALO) % (2 * NLON_OUT)

    def one_row(row):
        rows_here = lax.dynamic_slice_in_dim(padded, (2 * row).astype(jnp.int32), 5, axis=1)
        picked = rows_here[:, :, lon_index]
        return jnp.einsum('crjd,krd->kcj', picked, masked32[row], precision=lax.Precision.HIGHEST)
    return lax.map(one_row, jnp.arange(NLAT_OUT, dtype=jnp.int32))

def reference(field_in, filter_weight, filter_basis, halo_reach, grad_out):
    offsets = jnp.abs(jnp.arange(2 * HALO + 1, dtype=jnp.int32) - HALO)
    keep = (offsets[None, :] <= halo_reach[:, None]).astype(jnp.float32)
    masked32 = filter_basis.astype(jnp.float32) * keep[:, None, None, :]
    field32 = field_in.astype(jnp.float32)
    inner = lax.optimization_barrier(stencil(field32, masked32).astype(jnp.bfloat16)).astype(jnp.float32)
    weight32 = filter_weight.astype(jnp.float32)
    field_out = jnp.einsum('okc,ikcj->oij', weight32, inner, precision=lax.Precision.HIGHEST).astype(jnp.bfloat16)
    cotangent = grad_out.astype(jnp.float32)
    factor = 1.0 / math.sqrt(NLAT_OUT * NLON_OUT)
    grad_weight = jnp.einsum('oij,ikcj->okc', cotangent, inner, precision=lax.Precision.HIGHEST) * factor
    grad_inner = jnp.einsum('okc,oij->ikcj', weight32, cotangent, precision=lax.Precision.HIGHEST)
    grad_inner = lax.optimization_barrier(grad_inner.astype(jnp.bfloat16)).astype(jnp.float32)
    unused, pullback = jax.vjp(lambda field: stencil(field, masked32), field32)
    grad_in = pullback(grad_inner)[0].astype(jnp.bfloat16)
    return (field_out, grad_in, grad_weight)
```

```python
import functools
import math

import jax
import jax.numpy as jnp
import numpy as np
from jax import lax
from jax.experimental import pallas as pl
from jax.experimental.pallas import tpu as pltpu
from jax.sharding import PartitionSpec as P

BF16 = jnp.bfloat16
F32 = jnp.float32
OUT_BLOCK = 48
BACK_BLOCK = 32
VMEM_LIMIT = 56 * 2**20


def shifted(shard, axis, by):
    size = lax.axis_size(axis)
    pairs = [(i, i + by) for i in range(size) if 0 <= i + by < size]
    return lax.ppermute(shard, axis, pairs)


def masked_basis(filter_basis, halo_reach):
    halo = filter_basis.shape[3] // 2
    offsets = jnp.abs(lax.iota(jnp.int32, filter_basis.shape[3]) - halo)
    keep = (offsets[None, :] <= halo_reach[:, None]).astype(filter_basis.dtype)
    return filter_basis * keep[:, None, None, :]


def forward_matrix(masked):
    count, kernels, rows, taps = masked.shape
    span = 2 * OUT_BLOCK + taps - 1
    table = np.arange(span) == 2 * np.arange(OUT_BLOCK)[:, None] + np.arange(taps)[:, None, None]
    table = jnp.asarray(table.reshape(taps, -1), BF16)
    spread = jnp.dot(masked.reshape(-1, taps), table, preferred_element_type=F32).astype(BF16)
    spread = spread.reshape(count, kernels, rows, OUT_BLOCK, span).transpose(0, 1, 3, 2, 4)
    return spread.reshape(count, kernels * OUT_BLOCK, rows * span)


def backward_pairs(count, rows):
    reach = rows // 2
    return [
        (q, i + 1, q - 2 * i + reach)
        for i in range(-1, count + 1)
        for q in range(2 * count)
        if 0 <= q - 2 * i + reach < rows
    ]


def backward_matrix(masked, pairs):
    kernels, taps = masked.shape[1], masked.shape[3]
    span = BACK_BLOCK + taps // 2
    lag = np.arange(2 * BACK_BLOCK)[:, None] - 2 * np.arange(span) + taps - 1
    table = jnp.asarray((lag == np.arange(taps)[:, None, None]).reshape(taps, -1), BF16)
    picked = jnp.stack([masked[i, :, r] for _, i, r in pairs])
    spread = jnp.dot(picked.reshape(-1, taps), table, preferred_element_type=F32).astype(BF16)
    spread = spread.reshape(len(pairs), kernels, 2 * BACK_BLOCK, span).transpose(0, 2, 1, 3)
    return spread.reshape(len(pairs) * 2 * BACK_BLOCK, kernels * span)


def forward_kernel(kernels, halo, factor, own, below, above, mats, grad, inner, weight, ext):
    rows, width, chans = own.shape
    count, _, depth = mats.shape
    lat = ext.shape[0] - rows + 2
    before, after = below.shape[0], above.shape[0]
    ext[:before, halo : halo + width] = below[...]
    ext[before : before + rows, halo : halo + width] = own[...]
    ext[before + rows :, halo : halo + width] = above[...]
    ext[:, :halo] = ext[:, width : width + halo]
    ext[:, halo + width :] = ext[:, halo : 2 * halo]
    out_width = width // 2
    span = depth // lat

    for i in range(count):

        def block(b, carry, i=i):
            start = pl.multiple_of(b * 2 * OUT_BLOCK, 32)
            window = ext[2 * i : 2 * i + lat, pl.ds(start, span), :].reshape(depth, chans)
            got = jnp.dot(mats[i], window, preferred_element_type=F32).astype(BF16)
            to = pl.multiple_of(i * out_width + b * OUT_BLOCK, 16)
            for k in range(kernels):
                piece = got[k * OUT_BLOCK : (k + 1) * OUT_BLOCK]
                inner[pl.ds(to, OUT_BLOCK), k * chans : (k + 1) * chans] = piece
            return carry

        lax.fori_loop(0, out_width // OUT_BLOCK, block, 0)

    def column(k, carry):
        at = pl.ds(pl.multiple_of(k * chans, chans), chans)
        weight[:, at] = jnp.dot(grad[...], inner[:, at], preferred_element_type=F32) * factor
        return carry

    lax.fori_loop(0, kernels, column, 0)


def mix_kernel(mixer, inner, out):
    total = inner.shape[0]
    for at in range(0, total, 256):
        to = min(at + 256, total)
        got = lax.dot_general(
            mixer[...], inner[at:to], (((1,), (1,)), ((), ())), preferred_element_type=F32
        )
        out[:, at:to] = got.astype(BF16)


def backward_kernel(kernels, pairs, grads, mixer, mats, out, held):
    nrows, length, _ = grads.shape
    chans = mixer.shape[1] // kernels
    span = mats.shape[1] // kernels
    step = 2 * BACK_BLOCK
    for i in range(nrows):

        def column(k, carry, i=i):
            at = pl.ds(pl.multiple_of(k * chans, chans), chans)
            got = jnp.dot(grads[i], mixer[:, at], preferred_element_type=F32)
            held[i, :, at] = got.astype(BF16)
            return carry

        lax.fori_loop(0, kernels, column, 0)

    def block(b, carry):
        start = pl.multiple_of(b * BACK_BLOCK, 16)
        sums = [None] * out.shape[0]
        for i in range(nrows):
            mine = [n for n, p in enumerate(pairs) if p[1] == i]
            window = jnp.concatenate(
                [held[i, pl.ds(start, span), k * chans : (k + 1) * chans] for k in range(kernels)], 0
            )
            left = mats[mine[0] * step : (mine[-1] + 1) * step]
            got = jnp.dot(left, window, preferred_element_type=F32)
            for n, m in enumerate(mine):
                q = pairs[m][0]
                term = got[n * step : (n + 1) * step]
                sums[q] = term if sums[q] is None else sums[q] + term
        for q, value in enumerate(sums):
            out[q, pl.ds(pl.multiple_of(b * step, 32), step), :] = value.astype(BF16)
        return carry

    lax.fori_loop(0, out.shape[1] // step, block, 0)


def call(body, out_shape, scratch, flops, *args):
    n_bytes = sum(a.size * a.dtype.itemsize for a in args)
    whole = pl.BlockSpec(memory_space=pltpu.VMEM)
    return pl.pallas_call(
        body,
        out_shape=out_shape,
        in_specs=[whole] * len(args),
        out_specs=jax.tree.map(lambda _: whole, out_shape),
        scratch_shapes=scratch,
        compiler_params=pltpu.CompilerParams(vmem_limit_bytes=VMEM_LIMIT),
        cost_estimate=pl.CostEstimate(flops=flops, bytes_accessed=n_bytes, transcendentals=0),
    )(*args)


def summed(term, axis):
    size = lax.axis_size(axis)
    steps = size.bit_length() - 1
    if size != 1 << steps or term.shape[0] % size:
        return lax.psum(term, axis)
    me = lax.axis_index(axis)
    for bit in range(steps):
        half = term.shape[0] // 2
        pairs = [(i, i ^ (1 << bit)) for i in range(size)]
        high = (me >> bit) & 1
        sent = lax.dynamic_slice_in_dim(term, (1 - high) * half, half, 0).astype(BF16)
        kept = lax.dynamic_slice_in_dim(term, high * half, half, 0)
        term = kept + lax.ppermute(sent, axis, pairs).astype(F32)
    held = term.astype(BF16)
    for bit in reversed(range(steps)):
        pairs = [(i, i ^ (1 << bit)) for i in range(size)]
        high = ((me >> bit) & 1) == 1
        other = lax.ppermute(held, axis, pairs)
        held = jnp.concatenate(
            [jnp.where(high, other, held), jnp.where(high, held, other)], 0
        )
    return held.astype(F32)


def on_device(field_in, filter_weight, filter_basis, halo_reach, grad_out):
    chans, rows_own, width = field_in.shape
    outs, kernels, _ = filter_weight.shape
    count, out_width = grad_out.shape[1:]
    lat, taps = filter_basis.shape[2:]
    halo = taps // 2
    sds = jax.ShapeDtypeStruct

    own = field_in.transpose(1, 2, 0)
    below = shifted(own[rows_own - 2 :], "lat", 1)
    above = shifted(own[:1], "lat", -1)
    grads = grad_out.transpose(1, 2, 0)
    grad_below = shifted(grads[count - 1 :], "lat", 1)
    grad_above = shifted(grads[:1], "lat", -1)
    masked = masked_basis(filter_basis, halo_reach)
    masked_below = shifted(masked[count - 1 :], "lat", 1)
    masked_above = shifted(masked[:1], "lat", -1)
    mixer = filter_weight.reshape(outs, kernels * chans)

    factor = 1.0 / math.sqrt(lax.axis_size("lat") * count * out_width)
    total = count * out_width
    inner, weight_term = call(
        functools.partial(forward_kernel, kernels, halo, factor),
        (sds((total, kernels * chans), BF16), sds((outs, kernels * chans), F32)),
        [pltpu.VMEM((rows_own + 3, width + 2 * halo, chans), BF16)],
        10**10,
        own,
        below,
        above,
        forward_matrix(masked),
        grad_out.reshape(outs, total),
    )
    grad_weight = summed(weight_term, "lat").reshape(outs, kernels, chans)

    field_out = call(mix_kernel, sds((outs, total), BF16), [], 4 * 10**9, mixer, inner)
    field_out = field_out.reshape(outs, count, out_width)

    pairs = backward_pairs(count, lat)
    blocks = -(-out_width // BACK_BLOCK)
    span = BACK_BLOCK + halo
    length = (blocks - 1) * BACK_BLOCK + span
    lead = halo // 2
    all_grads = jnp.concatenate([grad_below, grads, grad_above], 0)
    all_grads = jnp.concatenate(
        [all_grads[:, out_width - lead :], all_grads, all_grads[:, : length - lead - out_width]], 1
    )
    all_masked = jnp.concatenate([masked_below, masked, masked_above], 0)
    back = call(
        functools.partial(backward_kernel, kernels, pairs),
        sds((rows_own, blocks * 2 * BACK_BLOCK, chans), BF16),
        [pltpu.VMEM((count + 2, length, kernels * chans), BF16)],
        14 * 10**9,
        all_grads,
        mixer,
        backward_matrix(all_masked, pairs),
    )
    grad_in = back[:, :width].transpose(2, 0, 1)
    return (field_out, grad_in, grad_weight)


def solution(mesh):
    return jax.shard_map(
        on_device,
        mesh=mesh,
        in_specs=(
            P("ens", "lat", None),
            P(),
            P("lat", None, None, None),
            P("lat"),
            P("ens", "lat", None),
        ),
        out_specs=(P("ens", "lat", None), P("ens", "lat", None), P("ens", None, None)),
        check_vma=False,
    )
```

```python
import functools
import math

import jax
import jax.numpy as jnp
import numpy as np
from jax import lax
from jax.experimental import pallas as pl
from jax.experimental.pallas import tpu as pltpu
from jax.sharding import PartitionSpec as P

BF16 = jnp.bfloat16
F32 = jnp.float32
OUT_BLOCK = 48
BACK_BLOCK = 32
MIX_PARTS = 6
VMEM_LIMIT = 56 * 2**20


def shifted(shard, axis, by):
    size = lax.axis_size(axis)
    pairs = [(i, i + by) for i in range(size) if 0 <= i + by < size]
    return lax.ppermute(shard, axis, pairs)


def masked_basis(filter_basis, halo_reach):
    halo = filter_basis.shape[3] // 2
    offsets = jnp.abs(lax.iota(jnp.int32, filter_basis.shape[3]) - halo)
    keep = (offsets[None, :] <= halo_reach[:, None]).astype(filter_basis.dtype)
    return filter_basis * keep[:, None, None, :]


def forward_matrix(masked):
    count, kernels, rows, taps = masked.shape
    span = 2 * OUT_BLOCK + taps - 1
    table = np.arange(span) == 2 * np.arange(OUT_BLOCK)[:, None] + np.arange(taps)[:, None, None]
    table = jnp.asarray(table.reshape(taps, -1), BF16)
    spread = jnp.dot(masked.reshape(-1, taps), table, preferred_element_type=F32).astype(BF16)
    spread = spread.reshape(count, kernels, rows, OUT_BLOCK, span).transpose(0, 1, 3, 2, 4)
    return spread.reshape(count, kernels * OUT_BLOCK, rows * span)


def backward_pairs(count, rows):
    reach = rows // 2
    return [
        (q, i + 1, q - 2 * i + reach)
        for i in range(-1, count + 1)
        for q in range(2 * count)
        if 0 <= q - 2 * i + reach < rows
    ]


def backward_matrix(masked, pairs):
    kernels, taps = masked.shape[1], masked.shape[3]
    span = BACK_BLOCK + taps // 2
    lag = np.arange(2 * BACK_BLOCK)[:, None] - 2 * np.arange(span) + taps - 1
    table = jnp.asarray((lag == np.arange(taps)[:, None, None]).reshape(taps, -1), BF16)
    picked = jnp.stack([masked[i, :, r] for _, i, r in pairs])
    spread = jnp.dot(picked.reshape(-1, taps), table, preferred_element_type=F32).astype(BF16)
    spread = spread.reshape(len(pairs), kernels, 2 * BACK_BLOCK, span).transpose(0, 2, 1, 3)
    return spread.reshape(len(pairs) * 2 * BACK_BLOCK, kernels * span)


def forward_kernel(kernels, halo, factor, own, below, above, mats, grad, inner, weight, ext):
    rows, width, chans = own.shape
    count, _, depth = mats.shape
    lat = ext.shape[0] - rows + 2
    before, after = below.shape[0], above.shape[0]
    ext[:before, halo : halo + width] = below[...]
    ext[before : before + rows, halo : halo + width] = own[...]
    ext[before + rows :, halo : halo + width] = above[...]
    ext[:, :halo] = ext[:, width : width + halo]
    ext[:, halo + width :] = ext[:, halo : 2 * halo]
    out_width = width // 2
    span = depth // lat

    for i in range(count):

        def block(b, carry, i=i):
            start = pl.multiple_of(b * 2 * OUT_BLOCK, 32)
            window = ext[2 * i : 2 * i + lat, pl.ds(start, span), :].reshape(depth, chans)
            got = jnp.dot(mats[i], window, preferred_element_type=F32).astype(BF16)
            to = pl.multiple_of(i * out_width + b * OUT_BLOCK, 16)
            for k in range(kernels):
                piece = got[k * OUT_BLOCK : (k + 1) * OUT_BLOCK]
                inner[pl.ds(to, OUT_BLOCK), k * chans : (k + 1) * chans] = piece
            return carry

        lax.fori_loop(0, out_width // OUT_BLOCK, block, 0)

    def column(k, carry):
        at = pl.ds(pl.multiple_of(k * chans, chans), chans)
        weight[k] = jnp.dot(grad[...], inner[:, at], preferred_element_type=F32) * factor
        return carry

    lax.fori_loop(0, kernels, column, 0)


def mix_kernel(mixer, inner, out, wide):
    kernels, _, chans = mixer.shape
    for k in range(kernels):
        wide[:, k * chans : (k + 1) * chans] = mixer[k]
    total = inner.shape[0]
    rows = total // MIX_PARTS

    def part(n, carry):
        at = pl.ds(pl.multiple_of(n * rows, 16), rows)
        got = lax.dot_general(
            inner[at], wide[...], (((1,), (1,)), ((), ())), preferred_element_type=F32
        )
        out[at] = got.astype(BF16)
        return carry

    lax.fori_loop(0, MIX_PARTS, part, 0)


def backward_kernel(kernels, pairs, grads, mixer, mats, out, held):
    nrows, length, _ = grads.shape
    chans = mixer.shape[2]
    span = mats.shape[1] // kernels
    step = 2 * BACK_BLOCK
    for i in range(nrows):

        def column(k, carry, i=i):
            at = pl.ds(pl.multiple_of(k * chans, chans), chans)
            got = jnp.dot(grads[i], mixer[k], preferred_element_type=F32)
            held[i, :, at] = got.astype(BF16)
            return carry

        lax.fori_loop(0, kernels, column, 0)

    width = out.shape[1]

    def block(b, size):
        start = pl.multiple_of(b * BACK_BLOCK, 16)
        sums = [None] * out.shape[0]
        for i in range(nrows):
            mine = [n for n, p in enumerate(pairs) if p[1] == i]
            window = jnp.concatenate(
                [held[i, pl.ds(start, span), k * chans : (k + 1) * chans] for k in range(kernels)], 0
            )
            left = mats[mine[0] * step : (mine[-1] + 1) * step]
            got = jnp.dot(left, window, preferred_element_type=F32)
            for n, m in enumerate(mine):
                q = pairs[m][0]
                term = got[n * step : (n + 1) * step]
                sums[q] = term if sums[q] is None else sums[q] + term
        for q, value in enumerate(sums):
            out[q, pl.ds(pl.multiple_of(b * step, 32), size), :] = value[:size].astype(BF16)

    def whole_block(b, carry):
        block(b, step)
        return carry

    lax.fori_loop(0, width // step, whole_block, 0)
    if width % step:
        block(width // step, width % step)


def call(body, out_shape, scratch, flops, *args):
    n_bytes = sum(a.size * a.dtype.itemsize for a in args)
    whole = pl.BlockSpec(memory_space=pltpu.VMEM)
    return pl.pallas_call(
        body,
        out_shape=out_shape,
        in_specs=[whole] * len(args),
        out_specs=jax.tree.map(lambda _: whole, out_shape),
        scratch_shapes=scratch,
        compiler_params=pltpu.CompilerParams(vmem_limit_bytes=VMEM_LIMIT),
        cost_estimate=pl.CostEstimate(flops=flops, bytes_accessed=n_bytes, transcendentals=0),
    )(*args)


def tied(value, *others):
    return lax.optimization_barrier((value, *others))


def summed(term, axis, work):
    size = lax.axis_size(axis)
    steps = size.bit_length() - 1
    if size != 1 << steps or term.shape[1] % size:
        return (lax.psum(term, axis), *(make(x) for make, x in work))
    me = lax.axis_index(axis)
    done = []
    for bit in range(steps):
        half = term.shape[1] // 2
        pairs = [(i, i ^ (1 << bit)) for i in range(size)]
        high = (me >> bit) & 1
        sent = lax.dynamic_slice_in_dim(term, (1 - high) * half, half, 1).astype(BF16)
        kept = lax.dynamic_slice_in_dim(term, high * half, half, 1)
        if bit > 0 and work:
            (make, given), work = work[0], work[1:]
            sent, given = tied(sent, given)
            other, made = tied(lax.ppermute(sent, axis, pairs), make(given))
            done.append(made)
        else:
            other = lax.ppermute(sent, axis, pairs)
        term = kept + other.astype(F32)
    held = term.astype(BF16)
    for bit in reversed(range(steps)):
        pairs = [(i, i ^ (1 << bit)) for i in range(size)]
        high = ((me >> bit) & 1) == 1
        other = lax.ppermute(held, axis, pairs)
        held = jnp.concatenate(
            [jnp.where(high, other, held), jnp.where(high, held, other)], 1
        )
    return (held.astype(F32), *done, *(make(x) for make, x in work))


def on_device(field_in, filter_weight, filter_basis, halo_reach, grad_out):
    chans, rows_own, width = field_in.shape
    outs, kernels, _ = filter_weight.shape
    count, out_width = grad_out.shape[1:]
    lat, taps = filter_basis.shape[2:]
    halo = taps // 2
    sds = jax.ShapeDtypeStruct

    own = field_in.transpose(1, 2, 0)
    below = shifted(own[rows_own - 2 :], "lat", 1)
    above = shifted(own[:1], "lat", -1)
    grads = grad_out.transpose(1, 2, 0)
    grad_below = shifted(grads[count - 1 :], "lat", 1)
    grad_above = shifted(grads[:1], "lat", -1)
    masked = masked_basis(filter_basis, halo_reach)
    masked_below = shifted(masked[count - 1 :], "lat", 1)
    masked_above = shifted(masked[:1], "lat", -1)
    mixer = filter_weight.transpose(1, 0, 2)

    factor = 1.0 / math.sqrt(lax.axis_size("lat") * count * out_width)
    total = count * out_width
    inner, weight_term = call(
        functools.partial(forward_kernel, kernels, halo, factor),
        (sds((total, kernels * chans), BF16), sds((kernels, outs, chans), F32)),
        [pltpu.VMEM((rows_own + 3, width + 2 * halo, chans), BF16)],
        10**10,
        own,
        below,
        above,
        forward_matrix(masked),
        grad_out.reshape(outs, total),
    )
    pairs = backward_pairs(count, lat)
    blocks = -(-out_width // BACK_BLOCK)
    span = BACK_BLOCK + halo
    length = (blocks - 1) * BACK_BLOCK + span
    lead = halo // 2
    all_grads = jnp.concatenate([grad_below, grads, grad_above], 0)
    all_grads = jnp.concatenate(
        [all_grads[:, out_width - lead :], all_grads, all_grads[:, : length - lead - out_width]], 1
    )
    all_masked = jnp.concatenate([masked_below, masked, masked_above], 0)
    back_mats = backward_matrix(all_masked, pairs)

    def mix(given):
        return call(
            mix_kernel,
            sds((total, outs), BF16),
            [pltpu.VMEM((outs, kernels * chans), BF16)],
            4 * 10**9,
            mixer,
            given,
        )

    def back(given):
        return call(
            functools.partial(backward_kernel, kernels, pairs),
            sds((rows_own, width, chans), BF16),
            [pltpu.VMEM((count + 2, length, kernels * chans), BF16)],
            14 * 10**9,
            given,
            mixer,
            back_mats,
        )

    grad_weight, grad_in, field_out = summed(
        weight_term, "lat", [(back, all_grads), (mix, inner)]
    )
    return (
        field_out.reshape(count, out_width, outs).transpose(2, 0, 1),
        grad_in.transpose(2, 0, 1),
        grad_weight.transpose(1, 0, 2),
    )


def solution(mesh):
    return jax.shard_map(
        on_device,
        mesh=mesh,
        in_specs=(
            P("ens", "lat", None),
            P(),
            P("lat", None, None, None),
            P("lat"),
            P("ens", "lat", None),
        ),
        out_specs=(P("ens", "lat", None), P("ens", "lat", None), P("ens", None, None)),
        check_vma=False,
    )
```

```python
import functools
import math

import jax
import jax.numpy as jnp
import numpy as np
from jax import lax
from jax.experimental import pallas as pl
from jax.experimental.pallas import tpu as pltpu
from jax.sharding import PartitionSpec as P

BF16 = jnp.bfloat16
F32 = jnp.float32
OUT_BLOCK = 48
BACK_BLOCK = 32
MIX_PARTS = 6
VMEM_LIMIT = 56 * 2**20


def shifted(shard, axis, by):
    size = lax.axis_size(axis)
    pairs = [(i, i + by) for i in range(size) if 0 <= i + by < size]
    return lax.ppermute(shard, axis, pairs)


def masked_basis(filter_basis, halo_reach):
    halo = filter_basis.shape[3] // 2
    offsets = jnp.abs(lax.iota(jnp.int32, filter_basis.shape[3]) - halo)
    keep = (offsets[None, :] <= halo_reach[:, None]).astype(filter_basis.dtype)
    return filter_basis * keep[:, None, None, :]


def forward_matrix(masked):
    count, kernels, rows, taps = masked.shape
    span = 2 * OUT_BLOCK + taps - 1
    table = np.arange(span) == 2 * np.arange(OUT_BLOCK)[:, None] + np.arange(taps)[:, None, None]
    table = jnp.asarray(table.reshape(taps, -1), BF16)
    spread = jnp.dot(masked.reshape(-1, taps), table, preferred_element_type=F32).astype(BF16)
    spread = spread.reshape(count, kernels, rows, OUT_BLOCK, span).transpose(0, 1, 3, 2, 4)
    return spread.reshape(count, kernels * OUT_BLOCK, rows * span)


def backward_pairs(count, rows):
    reach = rows // 2
    return [
        (q, i + 1, q - 2 * i + reach)
        for i in range(-1, count + 1)
        for q in range(2 * count)
        if 0 <= q - 2 * i + reach < rows
    ]


def backward_matrix(masked, pairs):
    kernels, taps = masked.shape[1], masked.shape[3]
    span = BACK_BLOCK + taps // 2
    lag = np.arange(2 * BACK_BLOCK)[:, None] - 2 * np.arange(span) + taps - 1
    table = jnp.asarray((lag == np.arange(taps)[:, None, None]).reshape(taps, -1), BF16)
    picked = jnp.stack([masked[i, :, r] for _, i, r in pairs])
    spread = jnp.dot(picked.reshape(-1, taps), table, preferred_element_type=F32).astype(BF16)
    spread = spread.reshape(len(pairs), kernels, 2 * BACK_BLOCK, span).transpose(0, 2, 1, 3)
    return spread.reshape(len(pairs) * 2 * BACK_BLOCK, kernels * span)


def forward_kernel(kernels, halo, factor, own, below, above, mats, grad, inner, weight, ext):
    rows, width, chans = own.shape
    count, _, depth = mats.shape
    lat = ext.shape[0] - rows + 2
    before, after = below.shape[0], above.shape[0]
    ext[:before, halo : halo + width] = below[...]
    ext[before : before + rows, halo : halo + width] = own[...]
    ext[before + rows :, halo : halo + width] = above[...]
    ext[:, :halo] = ext[:, width : width + halo]
    ext[:, halo + width :] = ext[:, halo : 2 * halo]
    out_width = width // 2
    span = depth // lat

    for i in range(count):

        def block(b, carry, i=i):
            start = pl.multiple_of(b * 2 * OUT_BLOCK, 32)
            window = ext[2 * i : 2 * i + lat, pl.ds(start, span), :].reshape(depth, chans)
            got = jnp.dot(mats[i], window, preferred_element_type=F32).astype(BF16)
            to = pl.multiple_of(i * out_width + b * OUT_BLOCK, 16)
            for k in range(kernels):
                piece = got[k * OUT_BLOCK : (k + 1) * OUT_BLOCK]
                inner[pl.ds(to, OUT_BLOCK), k * chans : (k + 1) * chans] = piece
            return carry

        lax.fori_loop(0, out_width // OUT_BLOCK, block, 0)

    def column(k, carry):
        at = pl.ds(pl.multiple_of(k * chans, chans), chans)
        weight[k] = jnp.dot(grad[...], inner[:, at], preferred_element_type=F32) * factor
        return carry

    lax.fori_loop(0, kernels, column, 0)


def exchange_kernel(
    kernels, pairs, size, term, inner, mixer, grads, mats,
    weight, field, back, held, wide, acc, sent, got, send_sem, recv_sem,
):
    steps = size.bit_length() - 1
    outs, chans = term.shape[1:]
    me = lax.axis_index("lat")
    bits = [lax.rem(me // (1 << s), 2) for s in range(steps)]
    partners = [me + (1 - 2 * bits[s]) * (1 << s) for s in range(steps)]
    halves = [outs >> (s + 1) for s in range(steps)]
    barrier = pltpu.get_barrier_semaphore()
    for partner in partners:
        pl.semaphore_signal(
            barrier, inc=1, device_id={"lat": partner}, device_id_type=pl.DeviceIdType.MESH
        )
    pl.semaphore_wait(barrier, steps)

    cut = (kernels + 1) // 2
    chunks = [slice(0, cut), slice(cut, kernels)]

    def place(first, s):
        return sum((bits[t] * halves[t] for t in range(first, s)), 0 * me)

    def rows(start, count):
        return pl.ds(pl.multiple_of(start, 16), count)

    def copy(c, t, source, target, s):
        made = pltpu.make_async_remote_copy(
            src_ref=source,
            dst_ref=target,
            send_sem=send_sem.at[c, t],
            recv_sem=recv_sem.at[c, t],
            device_id={"lat": partners[s]},
            device_id_type=pl.DeviceIdType.MESH,
        )
        made.start()
        return made

    def start(c, t):
        ks = chunks[c]
        if t < steps:
            h, lag = halves[t], outs - (outs >> t)
            source = term if t == 0 else acc
            away = rows(place(1, t) + (1 - bits[t]) * h, h)
            sent[ks, lag : lag + h] = source[ks, away].astype(BF16)
            return copy(c, t, sent.at[ks, lag : lag + h], got.at[ks, lag : lag + h], t)
        s = 2 * steps - 1 - t
        if t == steps:
            last = halves[-1]
            weight[ks, rows(place(0, steps), last)] = acc[ks, rows(place(1, steps), last)].astype(BF16)
        mine = weight.at[ks, rows(place(0, s + 1), halves[s])]
        return copy(c, t, mine, mine, s)

    def finish(c, t, made):
        ks = chunks[c]
        made.wait()
        if t < steps:
            h, lag = halves[t], outs - (outs >> t)
            arrived = got[ks, lag : lag + h].astype(F32)
            at = rows(place(1, t) + bits[t] * h, h)
            if t == 0:
                acc[ks] = term[ks, at] + arrived
            else:
                acc[ks, at] = acc[ks, at] + arrived

    units = back_units(kernels, pairs, grads, mixer, mats, back, held)
    units[4:4] = mix_units(mixer, inner, field, wide)
    flying = [start(c, 0) for c in range(2)]
    slots, done = 4 * steps, 0
    for t in range(2 * steps):
        for c in range(2):
            until = -(-len(units) * (2 * t + c + 1) // slots)
            for unit in units[done:until]:
                unit()
            done = until
            finish(c, t, flying[c])
            if t + 1 < 2 * steps:
                flying[c] = start(c, t + 1)


def mix_units(mixer, inner, out, wide):
    kernels, _, chans = mixer.shape
    rows = inner.shape[0] // MIX_PARTS

    def spread():
        for k in range(kernels):
            wide[:, k * chans : (k + 1) * chans] = mixer[k]

    def part(n):
        at = slice(n * rows, (n + 1) * rows)
        got = lax.dot_general(
            inner[at], wide[...], (((1,), (1,)), ((), ())), preferred_element_type=F32
        )
        out[at] = got.astype(BF16)

    return [spread] + [functools.partial(part, n) for n in range(MIX_PARTS)]


def back_units(kernels, pairs, grads, mixer, mats, out, held):
    nrows = grads.shape[0]
    chans = mixer.shape[2]
    span = mats.shape[1] // kernels
    step = 2 * BACK_BLOCK
    width = out.shape[1]

    def columns(i, first, last):
        def column(k, carry):
            at = pl.ds(pl.multiple_of(k * chans, chans), chans)
            held[i, :, at] = jnp.dot(grads[i], mixer[k], preferred_element_type=F32).astype(BF16)
            return carry

        lax.fori_loop(first, last, column, 0)

    def block(b, size):
        start = pl.multiple_of(b * BACK_BLOCK, 16)
        sums = [None] * out.shape[0]
        for i in range(nrows):
            mine = [n for n, p in enumerate(pairs) if p[1] == i]
            window = jnp.concatenate(
                [held[i, pl.ds(start, span), k * chans : (k + 1) * chans] for k in range(kernels)], 0
            )
            left = mats[mine[0] * step : (mine[-1] + 1) * step]
            got = jnp.dot(left, window, preferred_element_type=F32)
            for n, m in enumerate(mine):
                q = pairs[m][0]
                term = got[n * step : (n + 1) * step]
                sums[q] = term if sums[q] is None else sums[q] + term
        for q, value in enumerate(sums):
            out[q, pl.ds(pl.multiple_of(b * step, 32), size), :] = value[:size].astype(BF16)

    def blocks(first, last):
        def whole_block(b, carry):
            block(b, step)
            return carry

        lax.fori_loop(first, last, whole_block, 0)

    cut = (kernels + 1) // 2
    units = []
    for i in range(nrows):
        units.append(functools.partial(columns, i, 0, cut))
        units.append(functools.partial(columns, i, cut, kernels))
    full = width // step
    for first in range(0, full, 4):
        units.append(functools.partial(blocks, first, min(first + 4, full)))
    if width % step:
        units.append(functools.partial(block, full, width % step))
    return units


def call(body, out_shape, scratch, flops, *args, **params):
    n_bytes = sum(a.size * a.dtype.itemsize for a in args)
    whole = pl.BlockSpec(memory_space=pltpu.VMEM)
    return pl.pallas_call(
        body,
        out_shape=out_shape,
        in_specs=[whole] * len(args),
        out_specs=jax.tree.map(lambda _: whole, out_shape),
        scratch_shapes=scratch,
        compiler_params=pltpu.CompilerParams(vmem_limit_bytes=VMEM_LIMIT, **params),
        cost_estimate=pl.CostEstimate(flops=flops, bytes_accessed=n_bytes, transcendentals=0),
    )(*args)


def on_device(field_in, filter_weight, filter_basis, halo_reach, grad_out):
    chans, rows_own, width = field_in.shape
    outs, kernels, _ = filter_weight.shape
    count, out_width = grad_out.shape[1:]
    lat, taps = filter_basis.shape[2:]
    halo = taps // 2
    sds = jax.ShapeDtypeStruct

    own = field_in.transpose(1, 2, 0)
    below = shifted(own[rows_own - 2 :], "lat", 1)
    above = shifted(own[:1], "lat", -1)
    grads = grad_out.transpose(1, 2, 0)
    grad_below = shifted(grads[count - 1 :], "lat", 1)
    grad_above = shifted(grads[:1], "lat", -1)
    masked = masked_basis(filter_basis, halo_reach)
    masked_below = shifted(masked[count - 1 :], "lat", 1)
    masked_above = shifted(masked[:1], "lat", -1)
    mixer = filter_weight.transpose(1, 0, 2)

    factor = 1.0 / math.sqrt(lax.axis_size("lat") * count * out_width)
    total = count * out_width
    inner, weight_term = call(
        functools.partial(forward_kernel, kernels, halo, factor),
        (sds((total, kernels * chans), BF16), sds((kernels, outs, chans), F32)),
        [pltpu.VMEM((rows_own + 3, width + 2 * halo, chans), BF16)],
        10**10,
        own,
        below,
        above,
        forward_matrix(masked),
        grad_out.reshape(outs, total),
    )
    pairs = backward_pairs(count, lat)
    blocks = -(-out_width // BACK_BLOCK)
    span = BACK_BLOCK + halo
    length = (blocks - 1) * BACK_BLOCK + span
    lead = halo // 2
    all_grads = jnp.concatenate([grad_below, grads, grad_above], 0)
    all_grads = jnp.concatenate(
        [all_grads[:, out_width - lead :], all_grads, all_grads[:, : length - lead - out_width]], 1
    )
    all_masked = jnp.concatenate([masked_below, masked, masked_above], 0)
    back_mats = backward_matrix(all_masked, pairs)

    size = lax.axis_size("lat")
    steps = size.bit_length() - 1
    moved = outs - outs // size
    grad_weight, field_out, grad_in = call(
        functools.partial(exchange_kernel, kernels, pairs, size),
        (
            sds((kernels, outs, chans), BF16),
            sds((total, outs), BF16),
            sds((rows_own, width, chans), BF16),
        ),
        [
            pltpu.VMEM((count + 2, length, kernels * chans), BF16),
            pltpu.VMEM((outs, kernels * chans), BF16),
            pltpu.VMEM((kernels, outs // 2, chans), F32),
            pltpu.VMEM((kernels, moved, chans), BF16),
            pltpu.VMEM((kernels, moved, chans), BF16),
            pltpu.SemaphoreType.DMA((2, 2 * steps)),
            pltpu.SemaphoreType.DMA((2, 2 * steps)),
        ],
        18 * 10**9,
        weight_term,
        inner,
        mixer,
        all_grads,
        back_mats,
        collective_id=0,
        has_side_effects=True,
    )
    grad_weight = grad_weight.astype(F32)
    return (
        field_out.reshape(count, out_width, outs).transpose(2, 0, 1),
        grad_in.transpose(2, 0, 1),
        grad_weight.transpose(1, 0, 2),
    )


def solution(mesh):
    return jax.shard_map(
        on_device,
        mesh=mesh,
        in_specs=(
            P("ens", "lat", None),
            P(),
            P("lat", None, None, None),
            P("lat"),
            P("ens", "lat", None),
        ),
        out_specs=(P("ens", "lat", None), P("ens", "lat", None), P("ens", None, None)),
        check_vma=False,
    )
```

```python
import functools
import math

import jax
import jax.numpy as jnp
import numpy as np
from jax import lax
from jax.experimental import pallas as pl
from jax.experimental.pallas import tpu as pltpu
from jax.sharding import PartitionSpec as P

BF16 = jnp.bfloat16
F32 = jnp.float32
OUT_BLOCK = 48
BACK_BLOCK = 32
MIX_PARTS = 6
VMEM_LIMIT = 56 * 2**20


def shifted(shard, axis, by):
    size = lax.axis_size(axis)
    pairs = [(i, i + by) for i in range(size) if 0 <= i + by < size]
    return lax.ppermute(shard, axis, pairs)


def together(grads, masked, by):
    length, outs = grads.shape[1:]
    flat = masked.reshape(1, -1, masked.shape[3])
    depth, taps = flat.shape[1:]
    extra = jnp.pad(flat, ((0, 0), (0, -depth % 16), (0, outs - taps)))
    got = shifted(jnp.concatenate([grads, extra], 1), "lat", by)
    return got[:, :length], got[:, length : length + depth, :taps].reshape(masked.shape)


def masked_basis(filter_basis, halo_reach):
    halo = filter_basis.shape[3] // 2
    offsets = jnp.abs(lax.iota(jnp.int32, filter_basis.shape[3]) - halo)
    keep = (offsets[None, :] <= halo_reach[:, None]).astype(filter_basis.dtype)
    return filter_basis * keep[:, None, None, :]


def forward_matrix(masked):
    count, kernels, rows, taps = masked.shape
    span = 2 * OUT_BLOCK + taps - 1
    table = np.arange(span) == 2 * np.arange(OUT_BLOCK)[:, None] + np.arange(taps)[:, None, None]
    table = jnp.asarray(table.reshape(taps, -1), BF16)
    spread = jnp.dot(masked.reshape(-1, taps), table, preferred_element_type=F32).astype(BF16)
    spread = spread.reshape(count, kernels, rows, OUT_BLOCK, span).transpose(0, 1, 3, 2, 4)
    return spread.reshape(count, kernels * OUT_BLOCK, rows * span)


def backward_pairs(count, rows):
    reach = rows // 2
    return [
        (q, i + 1, q - 2 * i + reach)
        for i in range(-1, count + 1)
        for q in range(2 * count)
        if 0 <= q - 2 * i + reach < rows
    ]


def backward_matrix(masked, pairs):
    kernels, taps = masked.shape[1], masked.shape[3]
    span = BACK_BLOCK + taps // 2
    lag = np.arange(2 * BACK_BLOCK)[:, None] - 2 * np.arange(span) + taps - 1
    table = jnp.asarray((lag == np.arange(taps)[:, None, None]).reshape(taps, -1), BF16)
    picked = jnp.stack([masked[i, :, r] for _, i, r in pairs])
    spread = jnp.dot(picked.reshape(-1, taps), table, preferred_element_type=F32).astype(BF16)
    spread = spread.reshape(len(pairs), kernels, 2 * BACK_BLOCK, span).transpose(0, 2, 1, 3)
    return spread.reshape(len(pairs) * 2 * BACK_BLOCK, kernels * span)


def forward_kernel(kernels, halo, factor, own, below, above, mats, grad, inner, weight, ext):
    rows, width, chans = own.shape
    count, _, depth = mats.shape
    lat = ext.shape[0] - rows + 2
    before, after = below.shape[0], above.shape[0]
    ext[:before, halo : halo + width] = below[...]
    ext[before : before + rows, halo : halo + width] = own[...]
    ext[before + rows :, halo : halo + width] = above[...]
    ext[:, :halo] = ext[:, width : width + halo]
    ext[:, halo + width :] = ext[:, halo : 2 * halo]
    out_width = width // 2
    span = depth // lat

    for i in range(count):

        def block(b, carry, i=i):
            start = pl.multiple_of(b * 2 * OUT_BLOCK, 32)
            window = ext[2 * i : 2 * i + lat, pl.ds(start, span), :].reshape(depth, chans)
            got = jnp.dot(mats[i], window, preferred_element_type=F32).astype(BF16)
            to = pl.multiple_of(i * out_width + b * OUT_BLOCK, 16)
            for k in range(kernels):
                piece = got[k * OUT_BLOCK : (k + 1) * OUT_BLOCK]
                inner[pl.ds(to, OUT_BLOCK), k * chans : (k + 1) * chans] = piece
            return carry

        lax.fori_loop(0, out_width // OUT_BLOCK, block, 0)

    def column(k, carry):
        at = pl.ds(pl.multiple_of(k * chans, chans), chans)
        weight[k] = jnp.dot(grad[...], inner[:, at], preferred_element_type=F32) * factor
        return carry

    lax.fori_loop(0, kernels, column, 0)


def exchange_kernel(
    kernels, pairs, size, term, inner, mixer, grads, mats,
    weight, field, back, held, wide, acc, sent, got, send_sem, recv_sem,
):
    steps = size.bit_length() - 1
    outs, chans = term.shape[1:]
    me = lax.axis_index("lat")
    orders = [list(range(steps)), [0, *range(2, steps), 1][:steps]]
    bit_of = [lax.rem(me // (1 << s), 2) for s in range(steps)]
    partner_of = [me + (1 - 2 * bit_of[s]) * (1 << s) for s in range(steps)]
    halves = [outs >> (s + 1) for s in range(steps)]
    barrier = pltpu.get_barrier_semaphore()
    for partner in partner_of:
        pl.semaphore_signal(
            barrier, inc=1, device_id={"lat": partner}, device_id_type=pl.DeviceIdType.MESH
        )
    pl.semaphore_wait(barrier, steps)

    cut = (kernels + 1) // 2
    chunks = [slice(0, cut), slice(cut, kernels)]

    def bit(c, s):
        return bit_of[orders[c][s]]

    def place(c, first, s):
        return sum((bit(c, t) * halves[t] for t in range(first, s)), 0 * me)

    def rows(start, count):
        return pl.ds(pl.multiple_of(start, 16), count)

    def copy(c, t, source, target, s):
        made = pltpu.make_async_remote_copy(
            src_ref=source,
            dst_ref=target,
            send_sem=send_sem.at[c, t],
            recv_sem=recv_sem.at[c, t],
            device_id={"lat": partner_of[orders[c][s]]},
            device_id_type=pl.DeviceIdType.MESH,
        )
        made.start()
        return made

    def start(c, t):
        ks = chunks[c]
        if t < steps:
            h, lag = halves[t], outs - (outs >> t)
            source = term if t == 0 else acc
            away = rows(place(c, 1, t) + (1 - bit(c, t)) * h, h)
            sent[ks, lag : lag + h] = source[ks, away].astype(BF16)
            return copy(c, t, sent.at[ks, lag : lag + h], got.at[ks, lag : lag + h], t)
        s = 2 * steps - 1 - t
        if t == steps:
            last = halves[-1]
            own = acc[ks, rows(place(c, 1, steps), last)]
            weight[ks, rows(place(c, 0, steps), last)] = own.astype(BF16)
        mine = weight.at[ks, rows(place(c, 0, s + 1), halves[s])]
        return copy(c, t, mine, mine, s)

    def finish(c, t, made):
        ks = chunks[c]
        made.wait()
        if t < steps:
            h, lag = halves[t], outs - (outs >> t)
            arrived = got[ks, lag : lag + h].astype(F32)
            at = rows(place(c, 1, t) + bit(c, t) * h, h)
            if t == 0:
                acc[ks] = term[ks, at] + arrived
            else:
                acc[ks, at] = acc[ks, at] + arrived

    units = back_units(kernels, pairs, grads, mixer, mats, back, held)
    units[4:4] = mix_units(mixer, inner, field, wide)
    flying = [start(c, 0) for c in range(2)]
    slots, done = 4 * steps, 0
    for t in range(2 * steps):
        for c in range(2):
            until = -(-len(units) * (2 * t + c + 1) // slots)
            for unit in units[done:until]:
                unit()
            done = until
            finish(c, t, flying[c])
            if t + 1 < 2 * steps:
                flying[c] = start(c, t + 1)


def mix_units(mixer, inner, out, wide):
    kernels, _, chans = mixer.shape
    rows = inner.shape[0] // MIX_PARTS

    def spread():
        for k in range(kernels):
            wide[:, k * chans : (k + 1) * chans] = mixer[k]

    def part(n):
        at = slice(n * rows, (n + 1) * rows)
        got = lax.dot_general(
            inner[at], wide[...], (((1,), (1,)), ((), ())), preferred_element_type=F32
        )
        out[at] = got.astype(BF16)

    return [spread] + [functools.partial(part, n) for n in range(MIX_PARTS)]


def back_units(kernels, pairs, grads, mixer, mats, out, held):
    nrows = grads.shape[0]
    chans = mixer.shape[2]
    span = mats.shape[1] // kernels
    step = 2 * BACK_BLOCK
    width = out.shape[1]

    def columns(i, first, last):
        def column(k, carry):
            at = pl.ds(pl.multiple_of(k * chans, chans), chans)
            held[i, :, at] = jnp.dot(grads[i], mixer[k], preferred_element_type=F32).astype(BF16)
            return carry

        lax.fori_loop(first, last, column, 0)

    def block(b, size):
        start = pl.multiple_of(b * BACK_BLOCK, 16)
        sums = [None] * out.shape[0]
        for i in range(nrows):
            mine = [n for n, p in enumerate(pairs) if p[1] == i]
            window = jnp.concatenate(
                [held[i, pl.ds(start, span), k * chans : (k + 1) * chans] for k in range(kernels)], 0
            )
            left = mats[mine[0] * step : (mine[-1] + 1) * step]
            got = jnp.dot(left, window, preferred_element_type=F32)
            for n, m in enumerate(mine):
                q = pairs[m][0]
                term = got[n * step : (n + 1) * step]
                sums[q] = term if sums[q] is None else sums[q] + term
        for q, value in enumerate(sums):
            out[q, pl.ds(pl.multiple_of(b * step, 32), size), :] = value[:size].astype(BF16)

    def blocks(first, last):
        def whole_block(b, carry):
            block(b, step)
            return carry

        lax.fori_loop(first, last, whole_block, 0)

    cut = (kernels + 1) // 2
    units = []
    for i in range(nrows):
        units.append(functools.partial(columns, i, 0, cut))
        units.append(functools.partial(columns, i, cut, kernels))
    full = width // step
    for first in range(0, full, 4):
        units.append(functools.partial(blocks, first, min(first + 4, full)))
    if width % step:
        units.append(functools.partial(block, full, width % step))
    return units


def call(body, out_shape, scratch, flops, *args, **params):
    n_bytes = sum(a.size * a.dtype.itemsize for a in args)
    whole = pl.BlockSpec(memory_space=pltpu.VMEM)
    return pl.pallas_call(
        body,
        out_shape=out_shape,
        in_specs=[whole] * len(args),
        out_specs=jax.tree.map(lambda _: whole, out_shape),
        scratch_shapes=scratch,
        compiler_params=pltpu.CompilerParams(vmem_limit_bytes=VMEM_LIMIT, **params),
        cost_estimate=pl.CostEstimate(flops=flops, bytes_accessed=n_bytes, transcendentals=0),
    )(*args)


def on_device(field_in, filter_weight, filter_basis, halo_reach, grad_out):
    chans, rows_own, width = field_in.shape
    outs, kernels, _ = filter_weight.shape
    count, out_width = grad_out.shape[1:]
    lat, taps = filter_basis.shape[2:]
    halo = taps // 2
    sds = jax.ShapeDtypeStruct

    own = field_in.transpose(1, 2, 0)
    below = shifted(own[rows_own - 2 :], "lat", 1)
    above = shifted(own[:1], "lat", -1)
    grads = grad_out.transpose(1, 2, 0)
    masked = masked_basis(filter_basis, halo_reach)
    grad_below, masked_below = together(grads[count - 1 :], masked[count - 1 :], 1)
    grad_above, masked_above = together(grads[:1], masked[:1], -1)
    mixer = filter_weight.transpose(1, 0, 2)

    factor = 1.0 / math.sqrt(lax.axis_size("lat") * count * out_width)
    total = count * out_width
    inner, weight_term = call(
        functools.partial(forward_kernel, kernels, halo, factor),
        (sds((total, kernels * chans), BF16), sds((kernels, outs, chans), F32)),
        [pltpu.VMEM((rows_own + 3, width + 2 * halo, chans), BF16)],
        10**10,
        own,
        below,
        above,
        forward_matrix(masked),
        grad_out.reshape(outs, total),
    )
    pairs = backward_pairs(count, lat)
    blocks = -(-out_width // BACK_BLOCK)
    span = BACK_BLOCK + halo
    length = (blocks - 1) * BACK_BLOCK + span
    lead = halo // 2
    all_grads = jnp.concatenate([grad_below, grads, grad_above], 0)
    all_grads = jnp.concatenate(
        [all_grads[:, out_width - lead :], all_grads, all_grads[:, : length - lead - out_width]], 1
    )
    all_masked = jnp.concatenate([masked_below, masked, masked_above], 0)
    back_mats = backward_matrix(all_masked, pairs)

    size = lax.axis_size("lat")
    steps = size.bit_length() - 1
    moved = outs - outs // size
    grad_weight, field_out, grad_in = call(
        functools.partial(exchange_kernel, kernels, pairs, size),
        (
            sds((kernels, outs, chans), BF16),
            sds((total, outs), BF16),
            sds((rows_own, width, chans), BF16),
        ),
        [
            pltpu.VMEM((count + 2, length, kernels * chans), BF16),
            pltpu.VMEM((outs, kernels * chans), BF16),
            pltpu.VMEM((kernels, outs // 2, chans), F32),
            pltpu.VMEM((kernels, moved, chans), BF16),
            pltpu.VMEM((kernels, moved, chans), BF16),
            pltpu.SemaphoreType.DMA((2, 2 * steps)),
            pltpu.SemaphoreType.DMA((2, 2 * steps)),
        ],
        18 * 10**9,
        weight_term,
        inner,
        mixer,
        all_grads,
        back_mats,
        collective_id=0,
        has_side_effects=True,
    )
    grad_weight = grad_weight.astype(F32)
    return (
        field_out.reshape(count, out_width, outs).transpose(2, 0, 1),
        grad_in.transpose(2, 0, 1),
        grad_weight.transpose(1, 0, 2),
    )


def solution(mesh):
    return jax.shard_map(
        on_device,
        mesh=mesh,
        in_specs=(
            P("ens", "lat", None),
            P(),
            P("lat", None, None, None),
            P("lat"),
            P("ens", "lat", None),
        ),
        out_specs=(P("ens", "lat", None), P("ens", "lat", None), P("ens", None, None)),
        check_vma=False,
    )
```
